512 devices in a mesh: pair: 32 (over y, x), row: 16 (over z, core).
Axes of the slice: x: 4, y: 8, z: 8, core: 2. Of those that a mesh axis runs over, the one named last changes fastest.
Arguments:
- activations: float32 [32768, 8192], P('row', 'pair')
- lead: int32 [32], P('pair'), may hold values from 0 to 1
Outputs:
- rotated: float32 [32768, 8192], P('row', 'pair')
The draws below stay inside these ranges and needn't reach their ends.
All inputs are finite; a program needn't handle non-finite values.
Results may differ from the reference program's by a relative error of at most 0.00075.
Values sent between devices are 32-bit elements; how exact they have to be, the bound alone decides.
A program may use at most 64 MiB of HBM per device.

```python
import jax
import jax.numpy as jnp
from jax import lax

BLK = 128
ROUNDS = 6
NBLK = 64
COLS = 8192
ROWS = 32768


def draw_activations(key, part):
    key = jax.random.fold_in(key, 11)
    keys = jax.random.split(key, 6)
    rows_scale = jnp.exp(jax.random.uniform(keys[0], (ROWS, 1), jnp.float32, jnp.log(0.3), jnp.log(3.0)))
    cols_scale = jnp.exp(jax.random.uniform(keys[1], (1, COLS), jnp.float32, jnp.log(0.3), jnp.log(3.0)))
    common_row = jax.random.truncated_normal(keys[2], -4.0, 4.0, (ROWS, 1), jnp.float32)
    common_col = jax.random.truncated_normal(keys[3], -3.0, 3.0, (1, COLS), jnp.float32)
    ramp = 0.5 + jnp.arange(ROWS, dtype=jnp.float32)[:, None] / ROWS
    ramp = ramp * jnp.exp(jax.random.uniform(keys[4], (ROWS, 1), jnp.float32, -0.3, 0.3))
    noise = jax.random.truncated_normal(keys[5], -4.0, 4.0, (ROWS, COLS), jnp.float32)
    return rows_scale * cols_scale * (ramp * common_row * common_col + noise)


def touch_ends(entries, own_key, least, largest):
    shape = entries.shape
    spot = [jax.random.randint(jax.random.fold_in(own_key, axis), (), 0, shape[axis]) for axis in range(len(shape))]
    entries = entries.at[tuple(spot)].set(least)
    longest = shape.index(max(shape))
    spot[longest] = (spot[longest] + 1) % shape[longest]
    return entries.at[tuple(spot)].set(largest)


def setup_inputs(seed: int = 0) -> dict:
    key_list = jax.random.split(jax.random.key(seed), 3)
    return {
        "activations": draw_activations(jax.random.fold_in(key_list[2], 71), 0),
        "lead": touch_ends(jax.random.randint(key_list[1], (NBLK // 2,), 0, 2), jax.random.fold_in(key_list[1], 1), 0, 1).astype(jnp.int32),
    }


epsilon = 1e-06

def product(left, right):
    return jnp.dot(left.astype(jnp.float32), right.astype(jnp.float32), precision=lax.Precision.HIGHEST, preferred_element_type=jnp.float32)

def inverse_of(matrix):
    factor = jnp.linalg.cholesky(matrix)
    identity = jnp.eye(matrix.shape[0], dtype=matrix.dtype)
    return jax.scipy.linalg.cho_solve((factor, True), identity)

def rotation(coupling):
    width = coupling.shape[0]
    identity = jnp.eye(width, dtype=coupling.dtype)
    left_inverse = inverse_of(identity + product(coupling, coupling.T))
    right_inverse = inverse_of(identity + product(coupling.T, coupling))
    lead_column = jnp.concatenate([2.0 * left_inverse - identity, 2.0 * product(coupling.T, left_inverse)], axis=0)
    trail_column = jnp.concatenate([-2.0 * product(coupling, right_inverse), 2.0 * right_inverse - identity], axis=0)
    return (lead_column, trail_column)

def reference(activations, lead):
    pairs = lead.shape[0]
    blocks = activations.reshape(ROWS, pairs, 2, BLK).transpose(1, 2, 0, 3)
    swapped = (lead == 1)[:, None, None]
    leading = jnp.where(swapped, blocks[:, 1], blocks[:, 0])
    trailing = jnp.where(swapped, blocks[:, 0], blocks[:, 1])
    for sweep_round in range(ROUNDS):
        paired = jnp.concatenate([leading, trailing], axis=2)
        gram_cross = jnp.einsum('prb,prc->pbc', leading, trailing, precision=lax.Precision.HIGHEST)
        norms_lead = jnp.sum(leading * leading, axis=1)
        norms_trail = jnp.sum(trailing * trailing, axis=1)
        coupling = gram_cross / (norms_lead[:, :, None] + norms_trail[:, None, :] + epsilon)
        lead_column, trail_column = jax.vmap(rotation)(coupling)
        new_lead = jnp.einsum('prk,pkb->prb', paired, lead_column, precision=lax.Precision.HIGHEST)
        new_trail = jnp.einsum('prk,pkb->prb', paired, trail_column, precision=lax.Precision.HIGHEST)
        if sweep_round + 1 < ROUNDS:
            going_up = new_lead.at[0].set(new_trail[0])
            leading = jnp.concatenate([new_lead[:1], going_up[:-1]], axis=0)
            trailing = jnp.concatenate([new_trail[1:], new_lead[-1:]], axis=0)
        else:
            leading, trailing = (new_lead, new_trail)
    stacked = jnp.stack([leading, trailing], axis=1)
    return stacked.transpose(2, 0, 1, 3).reshape(ROWS, 2 * pairs * BLK)
```

```python
import functools

import jax
import jax.numpy as jnp
from jax import lax
from jax.experimental import pallas as pl
from jax.experimental.pallas import tpu as pltpu
from jax.sharding import PartitionSpec as P

ROUNDS = 6
EPSILON = 1e-06
STEPS = 8
CHUNKS = 8
MESH = pl.DeviceIdType.MESH
F32 = jnp.float32
BF16 = jnp.bfloat16


def dot(left, right, contract=((1,), (0,))):
    return lax.dot_general(
        left,
        right,
        (contract, ((), ())),
        precision=lax.Precision.HIGHEST if left.dtype == F32 else None,
        preferred_element_type=F32,
    )


def halves(value):
    high = value.astype(BF16)
    return high, (value - high.astype(F32)).astype(BF16)


def identity_of(width):
    rows = lax.broadcasted_iota(jnp.int32, (width, width), 0)
    columns = lax.broadcasted_iota(jnp.int32, (width, width), 1)
    return (rows == columns).astype(F32)


def inverses(matrices, bound, identity):
    scale = 2.0 / (1.0 + bound)
    gap = (bound - 1.0) / (bound + 1.0)
    rests = [identity - scale * matrix for matrix in matrices]
    found = [scale * identity for _ in matrices]
    for step in range(STEPS):
        factor = 2.0 / (2.0 - gap * gap)
        for i, rest in enumerate(rests):
            if step == 0:
                found[i] = factor * (scale * (identity + rest))
            else:
                found[i] = factor * (found[i] + dot(found[i], rest))
            if step + 1 < STEPS:
                rests[i] = (1.0 - factor) * identity + factor * dot(rest, rest)
        gap = gap * gap / (2.0 - gap * gap)
    for i, matrix in enumerate(matrices):
        found[i] = found[i] + dot(found[i], identity - dot(matrix, found[i]))
    return found


def rotation(coupling):
    identity = identity_of(coupling.shape[0])
    flipped = coupling.T
    bound = 1.0 + jnp.sum(coupling * coupling, keepdims=True)
    left, right = inverses(
        [identity + dot(coupling, flipped), identity + dot(flipped, coupling)], bound, identity
    )
    return (
        (2.0 * left - identity, -2.0 * dot(coupling, right)),
        (2.0 * dot(flipped, left), 2.0 * right - identity),
    )


def kernel(
    seats, group, lead_ref, act_ref, out_ref, held, stage, gram_out, gram_in, coup_out, coup_in,
    up_send, up_recv, down_send, down_recv, gram_send, gram_recv, coup_send, coup_recv,
):
    rows = act_ref.shape[0]
    width = act_ref.shape[1] // 2
    size = rows // CHUNKS
    band = width // group
    seat = lax.axis_index("pair")
    me = lax.axis_index("row")
    above = lax.rem(seat + 1, seats)
    below = lax.rem(seat + seats - 1, seats)
    swapped = lead_ref[0] == 1

    barrier = pltpu.get_barrier_semaphore()
    for step in range(1, group):
        pl.semaphore_signal(
            barrier, inc=1, device_id={"row": lax.rem(me + step, group)}, device_id_type=MESH
        )
    for condition, other in ((seat > 0, below), (seat < seats - 1, above)):
        @pl.when(condition)
        def _():
            pl.semaphore_signal(barrier, inc=1, device_id={"pair": other}, device_id_type=MESH)
    pl.semaphore_wait(
        barrier, group - 1 + (seat > 0).astype(jnp.int32) + (seat < seats - 1).astype(jnp.int32)
    )

    def part(c):
        return pl.ds(c * size, size)

    def up_copy(slot, c):
        return pltpu.make_async_remote_copy(
            src_ref=stage.at[0, part(c)], dst_ref=held.at[slot, 0, part(c)],
            send_sem=up_send.at[c], recv_sem=up_recv.at[slot, c],
            device_id={"pair": above}, device_id_type=MESH,
        )

    def down_copy(slot, c):
        return pltpu.make_async_remote_copy(
            src_ref=stage.at[1, part(c)], dst_ref=held.at[slot, 1, part(c)],
            send_sem=down_send.at[c], recv_sem=down_recv.at[slot, c],
            device_id={"pair": below}, device_id_type=MESH,
        )

    def gram_part(leading, trailing, totals):
        lead_high, lead_low = halves(leading)
        trail_high, trail_low = halves(trailing)
        both = dot(
            jnp.concatenate([lead_high, lead_low], axis=1),
            jnp.concatenate([trail_high, trail_low], axis=1),
            ((0,), (0,)),
        )
        cross = both[:width, :width] + (both[:width, width:] + both[width:, :width])
        norms = [
            jnp.sum((block * block).reshape(-1, 8, width), axis=0) for block in (leading, trailing)
        ]
        new = (cross, *norms)
        return new if totals is None else tuple(a + b for a, b in zip(totals, new))

    def coupling_of(cross, norm_lead, norm_trail):
        norm_lead = jnp.sum(norm_lead, axis=0, keepdims=True)
        norm_trail = jnp.sum(norm_trail, axis=0, keepdims=True)
        line = lax.broadcasted_iota(jnp.int32, (8, width), 0)
        norms = jnp.where(line == 0, norm_lead, jnp.where(line == 1, norm_trail, 0.0))
        for k in range(group):
            gram_out[k, :band] = cross[k * band : (k + 1) * band]
            gram_out[k, band:] = norms
        for step in range(1, group):
            other = lax.rem(me + step, group)
            pltpu.make_async_remote_copy(
                src_ref=gram_out.at[other], dst_ref=gram_in.at[step],
                send_sem=gram_send, recv_sem=gram_recv,
                device_id={"row": other}, device_id_type=MESH,
            ).start()
        total = gram_out[me]
        everything = pltpu.make_async_remote_copy(
            src_ref=gram_out.at[pl.ds(1, group - 1)], dst_ref=gram_in.at[pl.ds(1, group - 1)],
            send_sem=gram_send, recv_sem=gram_recv,
            device_id={"row": lax.rem(me + 1, group)}, device_id_type=MESH,
        )
        everything.wait_recv()
        for step in range(1, group):
            total = total + gram_in[step]
        lane = lax.broadcasted_iota(jnp.int32, (band, width), 1)
        own = lane == me * band + lax.broadcasted_iota(jnp.int32, (band, width), 0)
        column = jnp.sum(jnp.where(own, total[band : band + 1], 0.0), axis=1, keepdims=True)
        coup_out[...] = total[:band] / (column + total[band + 1 : band + 2] + EPSILON)
        for step in range(1, group):
            pltpu.make_async_remote_copy(
                src_ref=coup_out, dst_ref=coup_in.at[step],
                send_sem=coup_send, recv_sem=coup_recv,
                device_id={"row": lax.rem(me + step, group)}, device_id_type=MESH,
            ).start()
        coup_in[0] = coup_out[...]
        arrived = pltpu.make_async_remote_copy(
            src_ref=coup_in.at[pl.ds(1, group - 1)], dst_ref=coup_in.at[pl.ds(1, group - 1)],
            send_sem=coup_send, recv_sem=coup_recv,
            device_id={"row": lax.rem(me + 1, group)}, device_id_type=MESH,
        )
        arrived.wait_recv()
        coupling = jnp.concatenate(
            [coup_in[lax.rem(me - k + group, group)] for k in range(group)], axis=0
        )
        everything.wait_send()
        arrived.wait_send()
        return coupling

    def turn(coupling, swap_rows, swap_columns):
        (lead_lead, lead_trail), (trail_lead, trail_trail) = rotation(coupling)
        top = jnp.concatenate([lead_lead, lead_trail], axis=1)
        bottom = jnp.concatenate([trail_lead, trail_trail], axis=1)
        if swap_rows:
            top, bottom = jnp.where(swapped, bottom, top), jnp.where(swapped, top, bottom)
        whole = jnp.concatenate([top, bottom], axis=0)
        if swap_columns:
            turned = jnp.concatenate([whole[:, width:], whole[:, :width]], axis=1)
            whole = jnp.where(seat == 0, turned, whole)
        return halves(whole)

    def applied(block, turn_high, turn_low):
        high, low = halves(block)
        return dot(high, turn_high) + (dot(high, turn_low) + dot(low, turn_high))

    def apply_and_move(read, turned, slot):
        for c in range(CHUNKS):
            new = applied(read(c), *turned)
            stage[0, part(c)] = new[:, :width]
            stage[1, part(c)] = new[:, width:]

            @pl.when(seat < seats - 1)
            def _():
                up_copy(slot, c).start()

            @pl.when(seat == seats - 1)
            def _():
                held[slot, 1, part(c)] = new[:, :width]

            @pl.when(seat > 0)
            def _():
                down_copy(slot, c).start()

            @pl.when(seat == 0)
            def _():
                held[slot, 0, part(c)] = new[:, width:]

    def arrive(slot, c):
        @pl.when(seat > 0)
        def _():
            up_copy(slot, c).wait_recv()
            down_copy(slot, c).wait_send()

        @pl.when(seat < seats - 1)
        def _():
            down_copy(slot, c).wait_recv()
            up_copy(slot, c).wait_send()

    def moved_coupling(slot):
        totals = None
        for c in range(CHUNKS):
            arrive(slot, c)
            totals = gram_part(held[slot, 0, part(c)], held[slot, 1, part(c)], totals)
        return coupling_of(*totals)

    def held_block(slot, c):
        return jnp.concatenate([held[slot, 0, part(c)], held[slot, 1, part(c)]], axis=1)

    totals = None
    for c in range(CHUNKS):
        totals = gram_part(act_ref[part(c), :width], act_ref[part(c), width:], totals)
    cross, norm_first, norm_second = totals
    coupling = coupling_of(
        jnp.where(swapped, cross.T, cross),
        jnp.where(swapped, norm_second, norm_first),
        jnp.where(swapped, norm_first, norm_second),
    )
    apply_and_move(lambda c: act_ref[part(c)], turn(coupling, True, True), 0)

    def one_round(index, _):
        now = lax.rem(index - 1, 2)
        later = lax.rem(index, 2)
        coupling = moved_coupling(now)
        apply_and_move(lambda c: held_block(now, c), turn(coupling, False, True), later)
        return 0

    lax.fori_loop(1, ROUNDS - 1, one_round, 0)
    last = (ROUNDS - 2) % 2
    turned = turn(moved_coupling(last), False, False)
    for c in range(CHUNKS):
        out_ref[part(c)] = applied(held_block(last, c), *turned)


def shards(activations, lead):
    seats, group = lax.axis_size("pair"), lax.axis_size("row")
    rows, columns = activations.shape
    width = columns // 2
    band = width // group
    dma = pltpu.SemaphoreType.DMA
    return pl.pallas_call(
        functools.partial(kernel, seats, group),
        out_shape=jax.ShapeDtypeStruct((rows, columns), F32),
        in_specs=[
            pl.BlockSpec(memory_space=pltpu.SMEM),
            pl.BlockSpec(memory_space=pltpu.VMEM),
        ],
        out_specs=pl.BlockSpec(memory_space=pltpu.VMEM),
        scratch_shapes=[
            pltpu.VMEM((2, 2, rows, width), F32),
            pltpu.VMEM((2, rows, width), F32),
            pltpu.VMEM((group, band + 8, width), F32),
            pltpu.VMEM((group, band + 8, width), F32),
            pltpu.VMEM((band, width), F32),
            pltpu.VMEM((group, band, width), F32),
            dma((CHUNKS,)),
            dma((2, CHUNKS)),
            dma((CHUNKS,)),
            dma((2, CHUNKS)),
            dma,
            dma,
            dma,
            dma,
        ],
        compiler_params=pltpu.CompilerParams(
            collective_id=0, has_side_effects=True, vmem_limit_bytes=40 * 1024 * 1024
        ),
        cost_estimate=pl.CostEstimate(
            flops=ROUNDS * 2 * rows * columns * (columns + width),
            bytes_accessed=2 * rows * columns * 4,
            transcendentals=0,
        ),
    )(lead, activations)


def solution(mesh):
    return jax.shard_map(
        shards,
        mesh=mesh,
        in_specs=(P("row", "pair"), P("pair")),
        out_specs=P("row", "pair"),
        check_vma=False,
    )
```

```python
import functools

import jax
import jax.numpy as jnp
from jax import lax
from jax.experimental import pallas as pl
from jax.experimental.pallas import tpu as pltpu
from jax.sharding import PartitionSpec as P

ROUNDS = 6
EPSILON = 1e-06
STEPS = 8
CHUNKS = 8
MESH = pl.DeviceIdType.MESH
F32 = jnp.float32
BF16 = jnp.bfloat16


def dot(left, right, contract=((1,), (0,))):
    return lax.dot_general(
        left,
        right,
        (contract, ((), ())),
        precision=lax.Precision.HIGHEST if left.dtype == F32 else None,
        preferred_element_type=F32,
    )


def halves(value):
    high = value.astype(BF16)
    return high, (value - high.astype(F32)).astype(BF16)


def identity_of(width):
    rows = lax.broadcasted_iota(jnp.int32, (width, width), 0)
    columns = lax.broadcasted_iota(jnp.int32, (width, width), 1)
    return (rows == columns).astype(F32)


def inverses(matrices, bounds, identity):
    scales = [2.0 / (1.0 + bound) for bound in bounds]
    gaps = [(bound - 1.0) / (bound + 1.0) for bound in bounds]
    rests = [identity - scale * matrix for scale, matrix in zip(scales, matrices)]
    found = [scale * identity for scale in scales]
    for step in range(STEPS):
        for i, rest in enumerate(rests):
            factor = 2.0 / (2.0 - gaps[i] * gaps[i])
            if step == 0:
                found[i] = factor * (scales[i] * (identity + rest))
            else:
                found[i] = factor * (found[i] + dot(found[i], rest))
            if step + 1 < STEPS:
                rests[i] = (1.0 - factor) * identity + factor * dot(rest, rest)
            gaps[i] = gaps[i] * gaps[i] / (2.0 - gaps[i] * gaps[i])
    for i, matrix in enumerate(matrices):
        found[i] = found[i] + dot(found[i], identity - dot(matrix, found[i]))
    return found


def columns_of(lead_coupling, trail_coupling):
    identity = identity_of(lead_coupling.shape[0])
    lead_flipped, trail_flipped = lead_coupling.T, trail_coupling.T
    bounds = [
        1.0 + jnp.sum(coupling * coupling, keepdims=True)
        for coupling in (lead_coupling, trail_coupling)
    ]
    left, right = inverses(
        [
            identity + dot(lead_coupling, lead_flipped),
            identity + dot(trail_flipped, trail_coupling),
        ],
        bounds,
        identity,
    )
    return (
        (2.0 * left - identity, 2.0 * dot(lead_flipped, left)),
        (-2.0 * dot(trail_coupling, right), 2.0 * right - identity),
    )


def kernel(
    seats, group, lead_ref, act_ref, out_ref, held, raw, own, gram_out, gram_in, coup_out, coup_in,
    coup_own, coup_near, turn_own, up_send, up_recv, down_send, down_recv, raw_up_send, raw_up_recv,
    raw_down_send, raw_down_recv, near_up_send, near_up_recv, near_down_send, near_down_recv,
    gram_send, gram_recv, coup_send, coup_recv,
):
    rows = act_ref.shape[0]
    width = act_ref.shape[1] // 2
    size = rows // CHUNKS
    band = width // group
    seat = lax.axis_index("pair")
    me = lax.axis_index("row")
    above = lax.rem(seat + 1, seats)
    below = lax.rem(seat + seats - 1, seats)
    first, final = seat == 0, seat == seats - 1
    swapped = lead_ref[0] == 1

    barrier = pltpu.get_barrier_semaphore()
    for step in range(1, group):
        pl.semaphore_signal(
            barrier, inc=1, device_id={"row": lax.rem(me + step, group)}, device_id_type=MESH
        )
    for condition, other in ((seat > 0, below), (seat < seats - 1, above)):
        @pl.when(condition)
        def _():
            pl.semaphore_signal(barrier, inc=1, device_id={"pair": other}, device_id_type=MESH)
    pl.semaphore_wait(
        barrier, group - 1 + (seat > 0).astype(jnp.int32) + (seat < seats - 1).astype(jnp.int32)
    )

    def part(c):
        return pl.ds(c * size, size)

    def to(other, source, target, send, receive):
        return pltpu.make_async_remote_copy(
            src_ref=source, dst_ref=target, send_sem=send, recv_sem=receive,
            device_id={"pair": other}, device_id_type=MESH,
        )

    def up_copy(c):
        return to(above, own.at[0, 0, part(c)], held.at[0, 0, part(c)], up_send.at[c], up_recv.at[c])

    def down_copy(c):
        return to(
            below, own.at[0, 1, part(c)], held.at[0, 1, part(c)], down_send.at[c], down_recv.at[c]
        )

    def raw_up(slot, c):
        return to(
            above, held.at[slot, 0, part(c)], raw.at[slot, 0, part(c)],
            raw_up_send.at[c], raw_up_recv.at[slot, c],
        )

    def raw_down(slot, c):
        return to(
            below, held.at[slot, 1, part(c)], raw.at[slot, 1, part(c)],
            raw_down_send.at[c], raw_down_recv.at[slot, c],
        )

    def near_up(slot):
        return to(above, coup_own.at[slot], coup_near.at[slot, 0], near_up_send, near_up_recv.at[slot])

    def near_down(slot):
        return to(
            below, coup_own.at[slot], coup_near.at[slot, 1], near_down_send, near_down_recv.at[slot]
        )

    def gram_part(leading, trailing, totals):
        lead_high, lead_low = halves(leading)
        trail_high, trail_low = halves(trailing)
        both = dot(
            jnp.concatenate([lead_high, lead_low], axis=1),
            jnp.concatenate([trail_high, trail_low], axis=1),
            ((0,), (0,)),
        )
        cross = both[:width, :width] + (both[:width, width:] + both[width:, :width])
        norms = [
            jnp.sum((block * block).reshape(-1, 8, width), axis=0) for block in (leading, trailing)
        ]
        new = (cross, *norms)
        return new if totals is None else tuple(a + b for a, b in zip(totals, new))

    gram_all = pltpu.make_async_remote_copy(
        src_ref=gram_out.at[pl.ds(1, group - 1)], dst_ref=gram_in.at[pl.ds(1, group - 1)],
        send_sem=gram_send, recv_sem=gram_recv,
        device_id={"row": lax.rem(me + 1, group)}, device_id_type=MESH,
    )
    coup_all = pltpu.make_async_remote_copy(
        src_ref=coup_in.at[pl.ds(1, group - 1)], dst_ref=coup_in.at[pl.ds(1, group - 1)],
        send_sem=coup_send, recv_sem=coup_recv,
        device_id={"row": lax.rem(me + 1, group)}, device_id_type=MESH,
    )

    def sum_start(cross, norm_lead, norm_trail):
        norm_lead = jnp.sum(norm_lead, axis=0, keepdims=True)
        norm_trail = jnp.sum(norm_trail, axis=0, keepdims=True)
        line = lax.broadcasted_iota(jnp.int32, (8, width), 0)
        norms = jnp.where(line == 0, norm_lead, jnp.where(line == 1, norm_trail, 0.0))
        for k in range(group):
            gram_out[k, :band] = cross[k * band : (k + 1) * band]
            gram_out[k, band:] = norms
        for step in range(1, group):
            other = lax.rem(me + step, group)
            pltpu.make_async_remote_copy(
                src_ref=gram_out.at[other], dst_ref=gram_in.at[step],
                send_sem=gram_send, recv_sem=gram_recv,
                device_id={"row": other}, device_id_type=MESH,
            ).start()

    def sum_end():
        total = gram_out[me]
        gram_all.wait_recv()
        for step in range(1, group):
            total = total + gram_in[step]
        lane = lax.broadcasted_iota(jnp.int32, (band, width), 1)
        mine = lane == me * band + lax.broadcasted_iota(jnp.int32, (band, width), 0)
        column = jnp.sum(jnp.where(mine, total[band : band + 1], 0.0), axis=1, keepdims=True)
        coup_out[...] = total[:band] / (column + total[band + 1 : band + 2] + EPSILON)
        for step in range(1, group):
            pltpu.make_async_remote_copy(
                src_ref=coup_out, dst_ref=coup_in.at[step],
                send_sem=coup_send, recv_sem=coup_recv,
                device_id={"row": lax.rem(me + step, group)}, device_id_type=MESH,
            ).start()
        coup_in[0] = coup_out[...]
        coup_all.wait_recv()
        coupling = jnp.concatenate(
            [coup_in[lax.rem(me - k + group, group)] for k in range(group)], axis=0
        )
        gram_all.wait_send()
        coup_all.wait_send()
        return coupling

    def turn(coupling, swap_rows, swap_columns):
        lead_columns, trail_columns = columns_of(coupling, coupling)
        top, bottom = (
            jnp.concatenate(pair, axis=1) for pair in zip(lead_columns, trail_columns)
        )
        if swap_rows:
            top, bottom = jnp.where(swapped, bottom, top), jnp.where(swapped, top, bottom)
        whole = jnp.concatenate([top, bottom], axis=0)
        if swap_columns:
            turned = jnp.concatenate([whole[:, width:], whole[:, :width]], axis=1)
            whole = jnp.where(first, turned, whole)
        return halves(whole)

    def applied(block, turn_high, turn_low):
        high, low = halves(block)
        return dot(high, turn_high) + (dot(high, turn_low) + dot(low, turn_high))

    def applied_half(block, turn_both):
        high, low = halves(block)
        both = dot(high, turn_both)
        return both[:, :width] + (both[:, width:] + dot(low, turn_both[:, :width]))

    def held_block(slot, c):
        return jnp.concatenate([held[slot, 0, part(c)], held[slot, 1, part(c)]], axis=1)

    totals = None
    for c in range(CHUNKS):
        totals = gram_part(act_ref[part(c), :width], act_ref[part(c), width:], totals)
    cross, norm_first, norm_second = totals
    sum_start(
        jnp.where(swapped, cross.T, cross),
        jnp.where(swapped, norm_second, norm_first),
        jnp.where(swapped, norm_first, norm_second),
    )
    turned = turn(sum_end(), True, True)
    for c in range(CHUNKS):
        new = applied(act_ref[part(c)], *turned)
        own[0, 0, part(c)] = new[:, :width]
        own[0, 1, part(c)] = new[:, width:]

        @pl.when(seat < seats - 1)
        def _():
            up_copy(c).start()

        @pl.when(seat > 0)
        def _():
            down_copy(c).start()

        @pl.when(final)
        def _():
            held[0, 1, part(c)] = new[:, :width]

        @pl.when(first)
        def _():
            held[0, 0, part(c)] = new[:, width:]

    totals = None
    for c in range(CHUNKS):
        @pl.when(seat > 0)
        def _():
            up_copy(c).wait_recv()
            down_copy(c).wait_send()

        @pl.when(seat < seats - 1)
        def _():
            down_copy(c).wait_recv()
            up_copy(c).wait_send()

        leading, trailing = held[0, 0, part(c)], held[0, 1, part(c)]
        totals = gram_part(leading, trailing, totals)

        @pl.when(first)
        def _():
            raw[0, 0, part(c)] = leading
            own[0, 1, part(c)] = trailing

        @pl.when(final)
        def _():
            raw[0, 1, part(c)] = trailing
            own[0, 0, part(c)] = leading

    def forward(slot, c):
        @pl.when(seat < seats - 1)
        def _():
            raw_up(slot, c).start()

        @pl.when(seat > 0)
        def _():
            raw_down(slot, c).start()

    def one_round(index, totals):
        now = lax.rem(index, 2)
        later = 1 - now
        sum_start(*totals)

        @pl.when(index == 2)
        def _():
            for c in range(CHUNKS):
                forward(now, c)

        @pl.when(index > 2)
        def _():
            for c in range(CHUNKS):
                new = applied(held_block(later, c), turn_own[0], turn_own[1])
                own[now, 0, part(c)] = jnp.where(final, held[now, 0, part(c)], new[:, :width])
                own[now, 1, part(c)] = jnp.where(first, held[now, 1, part(c)], new[:, width:])

        coupling = sum_end()
        coup_own[now] = coupling

        @pl.when(seat < seats - 1)
        def _():
            near_up(now).start()

        @pl.when(seat > 0)
        def _():
            near_down(now).start()

        @pl.when(first)
        def _():
            coup_near[now, 0] = coupling

        @pl.when(final)
        def _():
            coup_near[now, 1] = coupling

        turn_own[0], turn_own[1] = turn(coupling, False, True)

        @pl.when(seat > 0)
        def _():
            near_up(now).wait_recv()
            near_down(now).wait_send()

        @pl.when(seat < seats - 1)
        def _():
            near_down(now).wait_recv()
            near_up(now).wait_send()

        low, high = coup_near[now, 0], coup_near[now, 1]
        (low_top, low_bottom), (high_top, high_bottom) = columns_of(
            jnp.where(seat == 1, -low.T, low), jnp.where(final, -high.T, high)
        )
        lead_turn = jnp.concatenate(
            [jnp.where(seat == 1, low_bottom, low_top), jnp.where(seat == 1, low_top, low_bottom)]
        )
        trail_turn = jnp.concatenate(
            [jnp.where(final, high_bottom, high_top), jnp.where(final, high_top, high_bottom)]
        )
        lead_turn = jnp.concatenate(halves(lead_turn), axis=1)
        trail_turn = jnp.concatenate(halves(trail_turn), axis=1)
        totals = None
        for c in range(CHUNKS):
            @pl.when(seat > 0)
            def _():
                raw_up(now, c).wait_recv()
                raw_down(now, c).wait_send()

            @pl.when(seat < seats - 1)
            def _():
                raw_down(now, c).wait_recv()
                raw_up(now, c).wait_send()

            leading = applied_half(
                jnp.concatenate([raw[now, 0, part(c)], own[now, 1, part(c)]], axis=1), lead_turn
            )
            trailing = applied_half(
                jnp.concatenate([own[now, 0, part(c)], raw[now, 1, part(c)]], axis=1), trail_turn
            )
            held[later, 0, part(c)] = leading
            held[later, 1, part(c)] = trailing

            @pl.when(index < ROUNDS - 1)
            def _():
                forward(later, c)

            @pl.when(first)
            def _():
                raw[later, 0, part(c)] = leading

            @pl.when(final)
            def _():
                raw[later, 1, part(c)] = trailing

            totals = gram_part(leading, trailing, totals)
        return totals

    totals = lax.fori_loop(2, ROUNDS, one_round, totals)
    last = ROUNDS % 2
    sum_start(*totals)
    turned = turn(sum_end(), False, False)
    for c in range(CHUNKS):
        out_ref[part(c)] = applied(held_block(last, c), *turned)


def shards(activations, lead):
    seats, group = lax.axis_size("pair"), lax.axis_size("row")
    rows, columns = activations.shape
    width = columns // 2
    band = width // group
    dma = pltpu.SemaphoreType.DMA
    return pl.pallas_call(
        functools.partial(kernel, seats, group),
        out_shape=jax.ShapeDtypeStruct((rows, columns), F32),
        in_specs=[
            pl.BlockSpec(memory_space=pltpu.SMEM),
            pl.BlockSpec(memory_space=pltpu.VMEM),
        ],
        out_specs=pl.BlockSpec(memory_space=pltpu.VMEM),
        scratch_shapes=[
            pltpu.VMEM((2, 2, rows, width), F32),
            pltpu.VMEM((2, 2, rows, width), F32),
            pltpu.VMEM((2, 2, rows, width), F32),
            pltpu.VMEM((group, band + 8, width), F32),
            pltpu.VMEM((group, band + 8, width), F32),
            pltpu.VMEM((band, width), F32),
            pltpu.VMEM((group, band, width), F32),
            pltpu.VMEM((2, width, width), F32),
            pltpu.VMEM((2, 2, width, width), F32),
            pltpu.VMEM((2, columns, columns), BF16),
            dma((CHUNKS,)),
            dma((CHUNKS,)),
            dma((CHUNKS,)),
            dma((CHUNKS,)),
            dma((CHUNKS,)),
            dma((2, CHUNKS)),
            dma((CHUNKS,)),
            dma((2, CHUNKS)),
            dma,
            dma((2,)),
            dma,
            dma((2,)),
            dma,
            dma,
            dma,
            dma,
        ],
        compiler_params=pltpu.CompilerParams(
            collective_id=0, has_side_effects=True, vmem_limit_bytes=48 * 1024 * 1024
        ),
        cost_estimate=pl.CostEstimate(
            flops=ROUNDS * 2 * rows * columns * (2 * columns + width),
            bytes_accessed=2 * rows * columns * 4,
            transcendentals=0,
        ),
    )(lead, activations)


def solution(mesh):
    return jax.shard_map(
        shards,
        mesh=mesh,
        in_specs=(P("row", "pair"), P("pair")),
        out_specs=P("row", "pair"),
        check_vma=False,
    )
```

```python
import functools

import jax
import jax.numpy as jnp
from jax import lax
from jax.experimental import pallas as pl
from jax.experimental.pallas import tpu as pltpu
from jax.sharding import PartitionSpec as P

ROUNDS = 6
EPSILON = 1e-06
STEPS = 8
CHUNKS = 8
EARLY = 4
AHEAD = 3
MESH = pl.DeviceIdType.MESH
F32 = jnp.float32
BF16 = jnp.bfloat16


def dot(left, right, contract=((1,), (0,))):
    return lax.dot_general(
        left,
        right,
        (contract, ((), ())),
        precision=lax.Precision.HIGHEST if left.dtype == F32 else None,
        preferred_element_type=F32,
    )


def halves(value):
    high = value.astype(BF16)
    return high, (value - high.astype(F32)).astype(BF16)


def identity_of(width):
    rows = lax.broadcasted_iota(jnp.int32, (width, width), 0)
    columns = lax.broadcasted_iota(jnp.int32, (width, width), 1)
    return (rows == columns).astype(F32)


def inverses(matrices, bounds, identity):
    scales = [2.0 / (1.0 + bound) for bound in bounds]
    gaps = [(bound - 1.0) / (bound + 1.0) for bound in bounds]
    rests = [identity - scale * matrix for scale, matrix in zip(scales, matrices)]
    found = [scale * identity for scale in scales]
    for step in range(STEPS):
        for i, rest in enumerate(rests):
            factor = 2.0 / (2.0 - gaps[i] * gaps[i])
            if step == 0:
                found[i] = factor * (scales[i] * (identity + rest))
            else:
                found[i] = factor * (found[i] + dot(found[i], rest))
            if step + 1 < STEPS:
                rests[i] = (1.0 - factor) * identity + factor * dot(rest, rest)
            gaps[i] = gaps[i] * gaps[i] / (2.0 - gaps[i] * gaps[i])
    for i, matrix in enumerate(matrices):
        found[i] = found[i] + dot(found[i], identity - dot(matrix, found[i]))
    return found


def columns_of(lead_coupling, trail_coupling):
    identity = identity_of(lead_coupling.shape[0])
    lead_flipped, trail_flipped = lead_coupling.T, trail_coupling.T
    bounds = [
        1.0 + jnp.sum(coupling * coupling, keepdims=True)
        for coupling in (lead_coupling, trail_coupling)
    ]
    left, right = inverses(
        [
            identity + dot(lead_coupling, lead_flipped),
            identity + dot(trail_flipped, trail_coupling),
        ],
        bounds,
        identity,
    )
    return (
        (2.0 * left - identity, 2.0 * dot(lead_flipped, left)),
        (-2.0 * dot(trail_coupling, right), 2.0 * right - identity),
    )


def kernel(
    seats, group, lead_ref, act_ref, out_ref, held, raw, own, gram_out, gram_in, coup_out, coup_in,
    coup_own, coup_near, up_send, up_recv, down_send, down_recv, raw_up_send, raw_up_recv,
    raw_down_send, raw_down_recv, ahead_up_send, ahead_up_recv, ahead_down_send, ahead_down_recv,
    near_up_send, near_up_recv, near_down_send, near_down_recv,
    gram_send, gram_recv, coup_send, coup_recv,
):
    rows = act_ref.shape[0]
    width = act_ref.shape[1] // 2
    size = rows // CHUNKS
    band = width // group
    seat = lax.axis_index("pair")
    me = lax.axis_index("row")
    above = lax.rem(seat + 1, seats)
    below = lax.rem(seat + seats - 1, seats)
    first, final = seat == 0, seat == seats - 1
    swapped = lead_ref[0] == 1

    barrier = pltpu.get_barrier_semaphore()
    for step in range(1, group):
        pl.semaphore_signal(
            barrier, inc=1, device_id={"row": lax.rem(me + step, group)}, device_id_type=MESH
        )
    for condition, other in ((seat > 0, below), (seat < seats - 1, above)):
        @pl.when(condition)
        def _():
            for step in range(group):
                pl.semaphore_signal(
                    barrier, inc=1, device_id={"pair": other, "row": lax.rem(me + step, group)},
                    device_id_type=MESH,
                )
    beside = (seat > 0).astype(jnp.int32) + (seat < seats - 1).astype(jnp.int32)
    pl.semaphore_wait(barrier, group - 1 + group * beside)
    far_first = sorted(range(group), key=lambda step: abs(2 * step - group))

    def part(c):
        return pl.ds(c * size, size)

    def to(other, source, target, send, receive):
        return pltpu.make_async_remote_copy(
            src_ref=source, dst_ref=target, send_sem=send, recv_sem=receive,
            device_id={"pair": other}, device_id_type=MESH,
        )

    def up_copy(c):
        return to(above, own.at[0, 0, part(c)], held.at[0, 0, part(c)], up_send.at[c], up_recv.at[c])

    def down_copy(c):
        return to(
            below, own.at[0, 1, part(c)], held.at[0, 1, part(c)], down_send.at[c], down_recv.at[c]
        )

    def raw_up(slot, c):
        return to(
            above, held.at[slot, 0, part(c)], raw.at[slot, 0, part(c)],
            raw_up_send.at[c], raw_up_recv.at[slot, c],
        )

    def raw_down(slot, c):
        return to(
            below, held.at[slot, 1, part(c)], raw.at[slot, 1, part(c)],
            raw_down_send.at[c], raw_down_recv.at[slot, c],
        )

    def ahead_up(c):
        return to(
            above, held.at[1, 1, part(c)], own.at[1, 1, part(c)], ahead_up_send.at[c], ahead_up_recv.at[c]
        )

    def ahead_down(c):
        return to(
            below, held.at[1, 0, part(c)], own.at[1, 0, part(c)],
            ahead_down_send.at[c], ahead_down_recv.at[c],
        )

    def near(other, side, slot, step, send, receive):
        return pltpu.make_async_remote_copy(
            src_ref=coup_out, dst_ref=coup_near.at[slot, side, step],
            send_sem=send, recv_sem=receive.at[slot],
            device_id={"pair": other, "row": lax.rem(me + step, group)}, device_id_type=MESH,
        )

    def near_all(other, side, slot, send, receive):
        return to(other, coup_near.at[slot, side], coup_near.at[slot, side], send, receive.at[slot])

    def gram_part(leading, trailing, totals):
        lead_high, lead_low = halves(leading)
        trail_high, trail_low = halves(trailing)
        both = dot(
            jnp.concatenate([lead_high, lead_low], axis=1),
            jnp.concatenate([trail_high, trail_low], axis=1),
            ((0,), (0,)),
        )
        cross = both[:width, :width] + (both[:width, width:] + both[width:, :width])
        norms = [
            jnp.sum((block * block).reshape(-1, 8, width), axis=0) for block in (leading, trailing)
        ]
        new = (cross, *norms)
        return new if totals is None else tuple(a + b for a, b in zip(totals, new))

    sent = pl.ds(0, band + 2)
    gram_all = pltpu.make_async_remote_copy(
        src_ref=gram_out.at[pl.ds(1, group - 1), sent], dst_ref=gram_in.at[pl.ds(1, group - 1), sent],
        send_sem=gram_send, recv_sem=gram_recv,
        device_id={"row": lax.rem(me + 1, group)}, device_id_type=MESH,
    )
    coup_all = pltpu.make_async_remote_copy(
        src_ref=coup_in.at[pl.ds(1, group - 1)], dst_ref=coup_in.at[pl.ds(1, group - 1)],
        send_sem=coup_send, recv_sem=coup_recv,
        device_id={"row": lax.rem(me + 1, group)}, device_id_type=MESH,
    )

    def sum_start(cross, norm_lead, norm_trail):
        norm_lead = jnp.sum(norm_lead, axis=0, keepdims=True)
        norm_trail = jnp.sum(norm_trail, axis=0, keepdims=True)
        line = lax.broadcasted_iota(jnp.int32, (8, width), 0)
        norms = jnp.where(line == 0, norm_lead, jnp.where(line == 1, norm_trail, 0.0))
        for k in range(group):
            gram_out[k, :band] = cross[k * band : (k + 1) * band]
            gram_out[k, band:] = norms
        for step in far_first[:-1]:
            other = lax.rem(me + step, group)
            pltpu.make_async_remote_copy(
                src_ref=gram_out.at[other, sent], dst_ref=gram_in.at[step, sent],
                send_sem=gram_send, recv_sem=gram_recv,
                device_id={"row": other}, device_id_type=MESH,
            ).start()

    def assembled(bands):
        return jnp.concatenate([bands[lax.rem(me - k + group, group)] for k in range(group)], axis=0)

    def sum_end(slot=None, late=False):
        total = gram_out[me, :band]
        norms = gram_out[me, band : band + 2]
        gram_all.wait_recv()
        for step in range(1, group):
            total = total + gram_in[step, :band]
            norms = norms + gram_in[step, band : band + 2]
        lane = lax.broadcasted_iota(jnp.int32, (band, width), 1)
        mine = lane == me * band + lax.broadcasted_iota(jnp.int32, (band, width), 0)
        column = jnp.sum(jnp.where(mine, norms[:1], 0.0), axis=1, keepdims=True)
        coup_out[...] = total / (column + norms[1:] + EPSILON)
        if slot is not None:
            for some in (far_first[: group // 2], far_first[group // 2 :]):
                @pl.when(seat < seats - 1)
                def _():
                    for step in some:
                        near(above, 0, slot, step, near_up_send, near_up_recv).start()

                @pl.when(seat > 0)
                def _():
                    for step in some:
                        near(below, 1, slot, step, near_down_send, near_down_recv).start()

        if late:
            forward(slot, EARLY)
        for step in far_first[:-1]:
            pltpu.make_async_remote_copy(
                src_ref=coup_out, dst_ref=coup_in.at[step],
                send_sem=coup_send, recv_sem=coup_recv,
                device_id={"row": lax.rem(me + step, group)}, device_id_type=MESH,
            ).start()
        if late:
            for c in range(EARLY + 1, CHUNKS):
                forward(slot, c)
        coup_in[0] = coup_out[...]
        coup_all.wait_recv()
        gram_all.wait_send()
        coup_all.wait_send()
        return assembled(coup_in)

    def turn(coupling, swap_rows, swap_columns):
        lead_columns, trail_columns = columns_of(coupling, coupling)
        top, bottom = (
            jnp.concatenate(pair, axis=1) for pair in zip(lead_columns, trail_columns)
        )
        if swap_rows:
            top, bottom = jnp.where(swapped, bottom, top), jnp.where(swapped, top, bottom)
        whole = jnp.concatenate([top, bottom], axis=0)
        if swap_columns:
            turned = jnp.concatenate([whole[:, width:], whole[:, :width]], axis=1)
            whole = jnp.where(first, turned, whole)
        return halves(whole)

    def applied(block, turn_high, turn_low):
        high, low = halves(block)
        return dot(high, turn_high) + (dot(high, turn_low) + dot(low, turn_high))

    def applied_half(block, turn_both):
        high, low = halves(block)
        both = dot(high, turn_both)
        return both[:, :width] + (both[:, width:] + dot(low, turn_both[:, :width]))

    def held_block(slot, c):
        return jnp.concatenate([held[slot, 0, part(c)], held[slot, 1, part(c)]], axis=1)

    def forward(slot, c):
        @pl.when(seat < seats - 1)
        def _():
            raw_up(slot, c).start()

        @pl.when(seat > 0)
        def _():
            raw_down(slot, c).start()

    def near_turns(now):
        @pl.when(first)
        def _():
            for step in range(group):
                coup_near[now, 0, step] = coup_in[step]

        @pl.when(final)
        def _():
            for step in range(group):
                coup_near[now, 1, step] = coup_in[step]

        @pl.when(seat > 0)
        def _():
            near_all(below, 0, now, near_down_send, near_up_recv).wait_recv()
            near_all(below, 1, now, near_down_send, near_down_recv).wait_send()

        @pl.when(seat < seats - 1)
        def _():
            near_all(above, 1, now, near_up_send, near_down_recv).wait_recv()
            near_all(above, 0, now, near_up_send, near_up_recv).wait_send()

        low, high = assembled(coup_near.at[now, 0]), assembled(coup_near.at[now, 1])
        (low_top, low_bottom), (high_top, high_bottom) = columns_of(
            jnp.where(seat == 1, -low.T, low), jnp.where(final, -high.T, high)
        )
        lead_turn = jnp.concatenate(
            [jnp.where(seat == 1, low_bottom, low_top), jnp.where(seat == 1, low_top, low_bottom)]
        )
        trail_turn = jnp.concatenate(
            [jnp.where(final, high_bottom, high_top), jnp.where(final, high_top, high_bottom)]
        )
        lead_turn = jnp.concatenate(halves(lead_turn), axis=1)
        trail_turn = jnp.concatenate(halves(trail_turn), axis=1)
        return lead_turn, trail_turn

    def near_chunk(now, c, turns):
        lead_turn, trail_turn = turns

        @pl.when(seat > 0)
        def _():
            raw_up(now, c).wait_recv()
            raw_down(now, c).wait_send()

        @pl.when(seat < seats - 1)
        def _():
            raw_down(now, c).wait_recv()
            raw_up(now, c).wait_send()

        leading = applied_half(
            jnp.concatenate([raw[now, 0, part(c)], own[now, 1, part(c)]], axis=1), lead_turn
        )
        trailing = applied_half(
            jnp.concatenate([own[now, 0, part(c)], raw[now, 1, part(c)]], axis=1), trail_turn
        )
        return leading, trailing

    def keep_at_ends(slot, c, leading, trailing):
        @pl.when(first)
        def _():
            raw[slot, 0, part(c)] = leading
            own[slot, 1, part(c)] = trailing

        @pl.when(final)
        def _():
            raw[slot, 1, part(c)] = trailing
            own[slot, 0, part(c)] = leading

    for c in range(AHEAD):
        one, two = act_ref[part(c), :width], act_ref[part(c), width:]
        leading, trailing = jnp.where(swapped, two, one), jnp.where(swapped, one, two)
        held[1, 0, part(c)] = leading
        held[1, 1, part(c)] = trailing
        forward(1, c)

        @pl.when(seat < seats - 1)
        def _():
            ahead_up(c).start()

        @pl.when(seat > 0)
        def _():
            ahead_down(c).start()

        keep_at_ends(1, c, leading, trailing)

    totals = None
    for c in range(CHUNKS):
        totals = gram_part(act_ref[part(c), :width], act_ref[part(c), width:], totals)
    cross, norm_first, norm_second = totals
    sum_start(
        jnp.where(swapped, cross.T, cross),
        jnp.where(swapped, norm_second, norm_first),
        jnp.where(swapped, norm_first, norm_second),
    )
    turned = turn(sum_end(1), True, True)
    for c in (*range(AHEAD, CHUNKS), *range(AHEAD)):
        new = applied(act_ref[part(c)], *turned)
        own[0, 0, part(c)] = new[:, :width]
        own[0, 1, part(c)] = new[:, width:]
        if c >= AHEAD:
            @pl.when(seat < seats - 1)
            def _():
                up_copy(c).start()

            @pl.when(seat > 0)
            def _():
                down_copy(c).start()

            @pl.when(final)
            def _():
                held[0, 1, part(c)] = new[:, :width]

            @pl.when(first)
            def _():
                held[0, 0, part(c)] = new[:, width:]

    turns = near_turns(1)
    totals = None
    for c in range(CHUNKS):
        if c < AHEAD:
            @pl.when(seat > 0)
            def _():
                ahead_up(c).wait_recv()
                ahead_down(c).wait_send()

            @pl.when(seat < seats - 1)
            def _():
                ahead_down(c).wait_recv()
                ahead_up(c).wait_send()

            leading, trailing = near_chunk(1, c, turns)
            held[0, 0, part(c)] = leading
            held[0, 1, part(c)] = trailing
        else:
            @pl.when(seat > 0)
            def _():
                up_copy(c).wait_recv()
                down_copy(c).wait_send()

            @pl.when(seat < seats - 1)
            def _():
                down_copy(c).wait_recv()
                up_copy(c).wait_send()

            leading, trailing = held[0, 0, part(c)], held[0, 1, part(c)]
        if c < EARLY:
            forward(0, c)
        totals = gram_part(leading, trailing, totals)
        keep_at_ends(0, c, leading, trailing)

    def one_round(index, totals):
        now = lax.rem(index, 2)
        later = 1 - now
        sum_start(*totals)

        @pl.when(index > 2)
        def _():
            turned = turn(coup_own[...], False, True)
            for c in range(CHUNKS):
                new = applied(held_block(later, c), *turned)
                own[now, 0, part(c)] = jnp.where(final, held[now, 0, part(c)], new[:, :width])
                own[now, 1, part(c)] = jnp.where(first, held[now, 1, part(c)], new[:, width:])

        coup_own[...] = sum_end(now, True)

        turns = near_turns(now)
        totals = None
        for c in range(CHUNKS):
            leading, trailing = near_chunk(now, c, turns)
            held[later, 0, part(c)] = leading
            held[later, 1, part(c)] = trailing

            if c < EARLY:
                @pl.when(index < ROUNDS - 1)
                def _():
                    forward(later, c)

            @pl.when(first)
            def _():
                raw[later, 0, part(c)] = leading

            @pl.when(final)
            def _():
                raw[later, 1, part(c)] = trailing

            totals = gram_part(leading, trailing, totals)
        return totals

    totals = lax.fori_loop(2, ROUNDS, one_round, totals)
    last = ROUNDS % 2
    sum_start(*totals)
    turned = turn(sum_end(), False, False)
    for c in range(CHUNKS):
        out_ref[part(c)] = applied(held_block(last, c), *turned)


def shards(activations, lead):
    seats, group = lax.axis_size("pair"), lax.axis_size("row")
    rows, columns = activations.shape
    width = columns // 2
    band = width // group
    dma = pltpu.SemaphoreType.DMA
    return pl.pallas_call(
        functools.partial(kernel, seats, group),
        out_shape=jax.ShapeDtypeStruct((rows, columns), F32),
        in_specs=[
            pl.BlockSpec(memory_space=pltpu.SMEM),
            pl.BlockSpec(memory_space=pltpu.VMEM),
        ],
        out_specs=pl.BlockSpec(memory_space=pltpu.VMEM),
        scratch_shapes=[
            pltpu.VMEM((2, 2, rows, width), F32),
            pltpu.VMEM((2, 2, rows, width), F32),
            pltpu.VMEM((2, 2, rows, width), F32),
            pltpu.VMEM((group, band + 8, width), F32),
            pltpu.VMEM((group, band + 8, width), F32),
            pltpu.VMEM((band, width), F32),
            pltpu.VMEM((group, band, width), F32),
            pltpu.VMEM((width, width), F32),
            pltpu.VMEM((2, 2, group, band, width), F32),
            dma((CHUNKS,)),
            dma((CHUNKS,)),
            dma((CHUNKS,)),
            dma((CHUNKS,)),
            dma((CHUNKS,)),
            dma((2, CHUNKS)),
            dma((CHUNKS,)),
            dma((2, CHUNKS)),
            dma((AHEAD,)),
            dma((AHEAD,)),
            dma((AHEAD,)),
            dma((AHEAD,)),
            dma,
            dma((2,)),
            dma,
            dma((2,)),
            dma,
            dma,
            dma,
            dma,
        ],
        compiler_params=pltpu.CompilerParams(
            collective_id=0, has_side_effects=True, vmem_limit_bytes=48 * 1024 * 1024
        ),
        cost_estimate=pl.CostEstimate(
            flops=ROUNDS * 2 * rows * columns * (2 * columns + width),
            bytes_accessed=2 * rows * columns * 4,
            transcendentals=0,
        ),
    )(lead, activations)


def solution(mesh):
    return jax.shard_map(
        shards,
        mesh=mesh,
        in_specs=(P("row", "pair"), P("pair")),
        out_specs=P("row", "pair"),
        check_vma=False,
    )
```

```python
import functools

import jax
import jax.numpy as jnp
from jax import lax
from jax.experimental import pallas as pl
from jax.experimental.pallas import tpu as pltpu
from jax.sharding import PartitionSpec as P

ROUNDS = 6
EPSILON = 1e-06
STEPS = 8
CHUNKS = 8
EARLY = 4
AHEAD = 2
MESH = pl.DeviceIdType.MESH
F32 = jnp.float32
BF16 = jnp.bfloat16


def dot(left, right, contract=((1,), (0,))):
    return lax.dot_general(
        left,
        right,
        (contract, ((), ())),
        precision=lax.Precision.HIGHEST if left.dtype == F32 else None,
        preferred_element_type=F32,
    )


def halves(value):
    high = value.astype(BF16)
    return high, (value - high.astype(F32)).astype(BF16)


def identity_of(width):
    rows = lax.broadcasted_iota(jnp.int32, (width, width), 0)
    columns = lax.broadcasted_iota(jnp.int32, (width, width), 1)
    return (rows == columns).astype(F32)


def inverses(matrices, bounds, identity):
    scales = [2.0 / (1.0 + bound) for bound in bounds]
    gaps = [(bound - 1.0) / (bound + 1.0) for bound in bounds]
    rests = [identity - scale * matrix for scale, matrix in zip(scales, matrices)]
    found = [scale * identity for scale in scales]
    for step in range(STEPS):
        for i, rest in enumerate(rests):
            factor = 2.0 / (2.0 - gaps[i] * gaps[i])
            if step == 0:
                found[i] = factor * (scales[i] * (identity + rest))
            else:
                found[i] = factor * (found[i] + dot(found[i], rest))
            if step + 1 < STEPS:
                rests[i] = (1.0 - factor) * identity + factor * dot(rest, rest)
            gaps[i] = gaps[i] * gaps[i] / (2.0 - gaps[i] * gaps[i])
    for i, matrix in enumerate(matrices):
        found[i] = found[i] + dot(found[i], identity - dot(matrix, found[i]))
    return found


def columns_of(lead_coupling, trail_coupling):
    identity = identity_of(lead_coupling.shape[0])
    lead_flipped, trail_flipped = lead_coupling.T, trail_coupling.T
    bounds = [
        1.0 + jnp.sum(coupling * coupling, keepdims=True)
        for coupling in (lead_coupling, trail_coupling)
    ]
    left, right = inverses(
        [
            identity + dot(lead_coupling, lead_flipped),
            identity + dot(trail_flipped, trail_coupling),
        ],
        bounds,
        identity,
    )
    return (
        (2.0 * left - identity, 2.0 * dot(lead_flipped, left)),
        (-2.0 * dot(trail_coupling, right), 2.0 * right - identity),
    )


def kernel(
    seats, group, lead_ref, act_ref, out_ref, held, raw, own, gram_out, gram_in, coup_out, coup_in,
    coup_own, coup_near, turn_own, up_send, up_recv, down_send, down_recv, raw_up_send, raw_up_recv,
    raw_down_send, raw_down_recv, ahead_up_send, ahead_up_recv, ahead_down_send, ahead_down_recv,
    near_up_send, near_up_recv, near_down_send, near_down_recv,
    gram_send, gram_recv, coup_send, coup_recv,
):
    rows = act_ref.shape[0]
    width = act_ref.shape[1] // 2
    early_rows = rows // 2
    sizes = [early_rows // EARLY] * EARLY + [(rows - early_rows) // (CHUNKS - EARLY)] * (CHUNKS - EARLY)
    spans = [pl.ds(sum(sizes[:c]), sizes[c]) for c in range(CHUNKS)]
    band = width // group
    seat = lax.axis_index("pair")
    me = lax.axis_index("row")
    above = lax.rem(seat + 1, seats)
    below = lax.rem(seat + seats - 1, seats)
    first, final = seat == 0, seat == seats - 1
    swapped = lead_ref[0] == 1

    barrier = pltpu.get_barrier_semaphore()
    far_first = sorted(range(group), key=lambda step: abs(2 * step - group))
    for step in far_first[:-1]:
        pl.semaphore_signal(
            barrier, inc=1, device_id={"row": lax.rem(me + step, group)}, device_id_type=MESH
        )
    for condition, other in ((seat > 0, below), (seat < seats - 1, above)):
        @pl.when(condition)
        def _():
            for step in far_first:
                pl.semaphore_signal(
                    barrier, inc=1, device_id={"pair": other, "row": lax.rem(me + step, group)},
                    device_id_type=MESH,
                )
    beside = (seat > 0).astype(jnp.int32) + (seat < seats - 1).astype(jnp.int32)

    def part(c):
        return spans[c]

    def to(other, source, target, send, receive):
        return pltpu.make_async_remote_copy(
            src_ref=source, dst_ref=target, send_sem=send, recv_sem=receive,
            device_id={"pair": other}, device_id_type=MESH,
        )

    def up_copy(c):
        return to(above, own.at[0, 0, part(c)], held.at[0, 0, part(c)], up_send.at[c], up_recv.at[c])

    def down_copy(c):
        return to(
            below, own.at[0, 1, part(c)], held.at[0, 1, part(c)], down_send.at[c], down_recv.at[c]
        )

    def raw_up(slot, c):
        return to(
            above, held.at[slot, 0, part(c)], raw.at[slot, 0, part(c)],
            raw_up_send.at[c], raw_up_recv.at[slot, c],
        )

    def raw_down(slot, c):
        return to(
            below, held.at[slot, 1, part(c)], raw.at[slot, 1, part(c)],
            raw_down_send.at[c], raw_down_recv.at[slot, c],
        )

    def ahead_up(c):
        return to(
            above, held.at[1, 1, part(c)], own.at[1, 1, part(c)], ahead_up_send.at[c], ahead_up_recv.at[c]
        )

    def ahead_down(c):
        return to(
            below, held.at[1, 0, part(c)], own.at[1, 0, part(c)],
            ahead_down_send.at[c], ahead_down_recv.at[c],
        )

    def near(other, side, slot, step, send, receive):
        return pltpu.make_async_remote_copy(
            src_ref=coup_out, dst_ref=coup_near.at[slot, side, step],
            send_sem=send, recv_sem=receive.at[slot],
            device_id={"pair": other, "row": lax.rem(me + step, group)}, device_id_type=MESH,
        )

    def near_all(other, side, slot, send, receive):
        return to(other, coup_near.at[slot, side], coup_near.at[slot, side], send, receive.at[slot])

    def gram_part(leading, trailing, totals):
        lead_high, lead_low = halves(leading)
        trail_high, trail_low = halves(trailing)
        both = dot(
            jnp.concatenate([lead_high, lead_low], axis=1),
            jnp.concatenate([trail_high, trail_low], axis=1),
            ((0,), (0,)),
        )
        cross = both[:width, :width] + (both[:width, width:] + both[width:, :width])
        norms = [
            jnp.sum((block * block).reshape(-1, 8, width), axis=0) for block in (leading, trailing)
        ]
        new = (cross, *norms)
        return new if totals is None else tuple(a + b for a, b in zip(totals, new))

    sent = pl.ds(0, band + 2)
    gram_all = pltpu.make_async_remote_copy(
        src_ref=gram_out.at[pl.ds(1, group - 1), sent], dst_ref=gram_in.at[pl.ds(1, group - 1), sent],
        send_sem=gram_send, recv_sem=gram_recv,
        device_id={"row": lax.rem(me + 1, group)}, device_id_type=MESH,
    )
    coup_all = pltpu.make_async_remote_copy(
        src_ref=coup_in.at[pl.ds(1, group - 1)], dst_ref=coup_in.at[pl.ds(1, group - 1)],
        send_sem=coup_send, recv_sem=coup_recv,
        device_id={"row": lax.rem(me + 1, group)}, device_id_type=MESH,
    )

    def sum_stage(cross, norm_lead, norm_trail):
        norm_lead = jnp.sum(norm_lead, axis=0, keepdims=True)
        norm_trail = jnp.sum(norm_trail, axis=0, keepdims=True)
        line = lax.broadcasted_iota(jnp.int32, (8, width), 0)
        norms = jnp.where(line == 0, norm_lead, jnp.where(line == 1, norm_trail, 0.0))
        for k in range(group):
            gram_out[k, :band] = cross[k * band : (k + 1) * band]
            gram_out[k, band:] = norms

    def sum_send():
        for step in far_first[:-1]:
            other = lax.rem(me + step, group)
            pltpu.make_async_remote_copy(
                src_ref=gram_out.at[other, sent], dst_ref=gram_in.at[step, sent],
                send_sem=gram_send, recv_sem=gram_recv,
                device_id={"row": other}, device_id_type=MESH,
            ).start()

    def assembled(bands):
        return jnp.concatenate([bands[lax.rem(me - k + group, group)] for k in range(group)], axis=0)

    def sum_end(slot=None, meanwhile=None):
        total = gram_out[me, :band]
        norms = gram_out[me, band : band + 2]
        gram_all.wait_recv()
        for step in range(1, group):
            total = total + gram_in[step, :band]
            norms = norms + gram_in[step, band : band + 2]
        lane = lax.broadcasted_iota(jnp.int32, (band, width), 1)
        mine = lane == me * band + lax.broadcasted_iota(jnp.int32, (band, width), 0)
        column = jnp.sum(jnp.where(mine, norms[:1], 0.0), axis=1, keepdims=True)
        coup_out[...] = total / (column + norms[1:] + EPSILON)
        if slot is not None:
            for some in (far_first[: group // 2], far_first[group // 2 :]):
                @pl.when(seat < seats - 1)
                def _():
                    for step in some:
                        near(above, 0, slot, step, near_up_send, near_up_recv).start()

                @pl.when(seat > 0)
                def _():
                    for step in some:
                        near(below, 1, slot, step, near_down_send, near_down_recv).start()

        if meanwhile is not None:
            forward(slot, EARLY)
        for step in far_first[:-1]:
            pltpu.make_async_remote_copy(
                src_ref=coup_out, dst_ref=coup_in.at[step],
                send_sem=coup_send, recv_sem=coup_recv,
                device_id={"row": lax.rem(me + step, group)}, device_id_type=MESH,
            ).start()
        if meanwhile is not None:
            for c in range(EARLY + 1, CHUNKS):
                forward(slot, c)
            meanwhile()
        coup_in[0] = coup_out[...]
        coup_all.wait_recv()
        gram_all.wait_send()
        coup_all.wait_send()
        return assembled(coup_in)

    def turn(coupling, swap_rows, swap_columns):
        lead_columns, trail_columns = columns_of(coupling, coupling)
        top, bottom = (
            jnp.concatenate(pair, axis=1) for pair in zip(lead_columns, trail_columns)
        )
        if swap_rows:
            top, bottom = jnp.where(swapped, bottom, top), jnp.where(swapped, top, bottom)
        whole = jnp.concatenate([top, bottom], axis=0)
        if swap_columns:
            turned = jnp.concatenate([whole[:, width:], whole[:, :width]], axis=1)
            whole = jnp.where(first, turned, whole)
        return halves(whole)

    def applied(block, turn_high, turn_low):
        high, low = halves(block)
        return dot(high, turn_high) + (dot(high, turn_low) + dot(low, turn_high))

    def applied_half(block, turn_both):
        high, low = halves(block)
        both = dot(high, turn_both)
        return both[:, :width] + (both[:, width:] + dot(low, turn_both[:, :width]))

    def held_block(slot, c):
        return jnp.concatenate([held[slot, 0, part(c)], held[slot, 1, part(c)]], axis=1)

    def forward(slot, c):
        @pl.when(seat < seats - 1)
        def _():
            raw_up(slot, c).start()

        @pl.when(seat > 0)
        def _():
            raw_down(slot, c).start()

    def near_turns(now):
        @pl.when(first)
        def _():
            for step in range(group):
                coup_near[now, 0, step] = coup_in[step]

        @pl.when(final)
        def _():
            for step in range(group):
                coup_near[now, 1, step] = coup_in[step]

        @pl.when(seat > 0)
        def _():
            near_all(below, 0, now, near_down_send, near_up_recv).wait_recv()
            near_all(below, 1, now, near_down_send, near_down_recv).wait_send()

        @pl.when(seat < seats - 1)
        def _():
            near_all(above, 1, now, near_up_send, near_down_recv).wait_recv()
            near_all(above, 0, now, near_up_send, near_up_recv).wait_send()

        low, high = assembled(coup_near.at[now, 0]), assembled(coup_near.at[now, 1])
        (low_top, low_bottom), (high_top, high_bottom) = columns_of(
            jnp.where(seat == 1, -low.T, low), jnp.where(final, -high.T, high)
        )
        lead_turn = jnp.concatenate(
            [jnp.where(seat == 1, low_bottom, low_top), jnp.where(seat == 1, low_top, low_bottom)]
        )
        trail_turn = jnp.concatenate(
            [jnp.where(final, high_bottom, high_top), jnp.where(final, high_top, high_bottom)]
        )
        lead_turn = jnp.concatenate(halves(lead_turn), axis=1)
        trail_turn = jnp.concatenate(halves(trail_turn), axis=1)
        return lead_turn, trail_turn

    def near_chunk(now, c, turns):
        lead_turn, trail_turn = turns

        @pl.when(seat > 0)
        def _():
            raw_up(now, c).wait_recv()
            raw_down(now, c).wait_send()

        @pl.when(seat < seats - 1)
        def _():
            raw_down(now, c).wait_recv()
            raw_up(now, c).wait_send()

        leading = applied_half(
            jnp.concatenate([raw[now, 0, part(c)], own[now, 1, part(c)]], axis=1), lead_turn
        )
        trailing = applied_half(
            jnp.concatenate([own[now, 0, part(c)], raw[now, 1, part(c)]], axis=1), trail_turn
        )
        return leading, trailing

    def keep_at_ends(slot, c, leading, trailing):
        @pl.when(first)
        def _():
            raw[slot, 0, part(c)] = leading
            own[slot, 1, part(c)] = trailing

        @pl.when(final)
        def _():
            raw[slot, 1, part(c)] = trailing
            own[slot, 0, part(c)] = leading

    totals = None
    for c in range(CHUNKS):
        totals = gram_part(act_ref[part(c), :width], act_ref[part(c), width:], totals)
    cross, norm_first, norm_second = totals
    sum_stage(
        jnp.where(swapped, cross.T, cross),
        jnp.where(swapped, norm_second, norm_first),
        jnp.where(swapped, norm_first, norm_second),
    )
    for c in range(AHEAD):
        one, two = act_ref[part(c), :width], act_ref[part(c), width:]
        leading, trailing = jnp.where(swapped, two, one), jnp.where(swapped, one, two)
        held[1, 0, part(c)] = leading
        held[1, 1, part(c)] = trailing
        keep_at_ends(1, c, leading, trailing)

    pl.semaphore_wait(barrier, group - 1 + group * beside)
    sum_send()
    for c in range(AHEAD):
        forward(1, c)

        @pl.when(seat < seats - 1)
        def _():
            ahead_up(c).start()

        @pl.when(seat > 0)
        def _():
            ahead_down(c).start()

    turned = turn(sum_end(1), True, True)
    for c in (*range(AHEAD, CHUNKS), *range(AHEAD)):
        new = applied(act_ref[part(c)], *turned)
        own[0, 0, part(c)] = new[:, :width]
        own[0, 1, part(c)] = new[:, width:]
        if c >= AHEAD:
            @pl.when(seat < seats - 1)
            def _():
                up_copy(c).start()

            @pl.when(seat > 0)
            def _():
                down_copy(c).start()

            @pl.when(final)
            def _():
                held[0, 1, part(c)] = new[:, :width]

            @pl.when(first)
            def _():
                held[0, 0, part(c)] = new[:, width:]

    turns = near_turns(1)
    totals = None
    for c in range(CHUNKS):
        if c < AHEAD:
            @pl.when(seat > 0)
            def _():
                ahead_up(c).wait_recv()
                ahead_down(c).wait_send()

            @pl.when(seat < seats - 1)
            def _():
                ahead_down(c).wait_recv()
                ahead_up(c).wait_send()

            leading, trailing = near_chunk(1, c, turns)
            held[0, 0, part(c)] = leading
            held[0, 1, part(c)] = trailing
        else:
            @pl.when(seat > 0)
            def _():
                up_copy(c).wait_recv()
                down_copy(c).wait_send()

            @pl.when(seat < seats - 1)
            def _():
                down_copy(c).wait_recv()
                up_copy(c).wait_send()

            leading, trailing = held[0, 0, part(c)], held[0, 1, part(c)]
        if c < EARLY:
            forward(0, c)
        totals = gram_part(leading, trailing, totals)
        keep_at_ends(0, c, leading, trailing)

    def one_round(index, totals):
        now = lax.rem(index, 2)
        later = 1 - now
        sum_stage(*totals)
        sum_send()

        @pl.when(index > 2)
        def _():
            turn_own[0], turn_own[1] = turn(coup_own[...], False, True)

        def own_blocks():
            @pl.when(index > 2)
            def _():
                for c in range(CHUNKS):
                    new = applied(held_block(later, c), turn_own[0], turn_own[1])
                    own[now, 0, part(c)] = jnp.where(final, held[now, 0, part(c)], new[:, :width])
                    own[now, 1, part(c)] = jnp.where(first, held[now, 1, part(c)], new[:, width:])

        coup_own[...] = sum_end(now, own_blocks)

        turns = near_turns(now)
        totals = None
        for c in range(CHUNKS):
            leading, trailing = near_chunk(now, c, turns)
            held[later, 0, part(c)] = leading
            held[later, 1, part(c)] = trailing

            if c < EARLY:
                @pl.when(index < ROUNDS - 1)
                def _():
                    forward(later, c)

            @pl.when(first)
            def _():
                raw[later, 0, part(c)] = leading

            @pl.when(final)
            def _():
                raw[later, 1, part(c)] = trailing

            totals = gram_part(leading, trailing, totals)
        return totals

    totals = lax.fori_loop(2, ROUNDS, one_round, totals)
    last = ROUNDS % 2
    sum_stage(*totals)
    sum_send()
    turned = turn(sum_end(), False, False)
    for c in range(CHUNKS):
        out_ref[part(c)] = applied(held_block(last, c), *turned)


def shards(activations, lead):
    seats, group = lax.axis_size("pair"), lax.axis_size("row")
    rows, columns = activations.shape
    width = columns // 2
    band = width // group
    dma = pltpu.SemaphoreType.DMA
    return pl.pallas_call(
        functools.partial(kernel, seats, group),
        out_shape=jax.ShapeDtypeStruct((rows, columns), F32),
        in_specs=[
            pl.BlockSpec(memory_space=pltpu.SMEM),
            pl.BlockSpec(memory_space=pltpu.VMEM),
        ],
        out_specs=pl.BlockSpec(memory_space=pltpu.VMEM),
        scratch_shapes=[
            pltpu.VMEM((2, 2, rows, width), F32),
            pltpu.VMEM((2, 2, rows, width), F32),
            pltpu.VMEM((2, 2, rows, width), F32),
            pltpu.VMEM((group, band + 8, width), F32),
            pltpu.VMEM((group, band + 8, width), F32),
            pltpu.VMEM((band, width), F32),
            pltpu.VMEM((group, band, width), F32),
            pltpu.VMEM((width, width), F32),
            pltpu.VMEM((2, 2, group, band, width), F32),
            pltpu.VMEM((2, columns, columns), BF16),
            dma((CHUNKS,)),
            dma((CHUNKS,)),
            dma((CHUNKS,)),
            dma((CHUNKS,)),
            dma((CHUNKS,)),
            dma((2, CHUNKS)),
            dma((CHUNKS,)),
            dma((2, CHUNKS)),
            dma((AHEAD,)),
            dma((AHEAD,)),
            dma((AHEAD,)),
            dma((AHEAD,)),
            dma,
            dma((2,)),
            dma,
            dma((2,)),
            dma,
            dma,
            dma,
            dma,
        ],
        compiler_params=pltpu.CompilerParams(
            collective_id=0, has_side_effects=True, vmem_limit_bytes=48 * 1024 * 1024
        ),
        cost_estimate=pl.CostEstimate(
            flops=ROUNDS * 2 * rows * columns * (2 * columns + width),
            bytes_accessed=2 * rows * columns * 4,
            transcendentals=0,
        ),
    )(lead, activations)


def solution(mesh):
    return jax.shard_map(
        shards,
        mesh=mesh,
        in_specs=(P("row", "pair"), P("pair")),
        out_specs=P("row", "pair"),
        check_vma=False,
    )
```

```python
import functools

import jax
import jax.numpy as jnp
from jax import lax
from jax.experimental import pallas as pl
from jax.experimental.pallas import tpu as pltpu
from jax.sharding import PartitionSpec as P

ROUNDS = 6
EPSILON = 1e-06
STEPS = 8
CHUNKS = 8
EARLY = 4
AHEAD = 2
MESH = pl.DeviceIdType.MESH
F32 = jnp.float32
BF16 = jnp.bfloat16


def dot(left, right, contract=((1,), (0,))):
    return lax.dot_general(
        left,
        right,
        (contract, ((), ())),
        precision=lax.Precision.HIGHEST if left.dtype == F32 else None,
        preferred_element_type=F32,
    )


def halves(value):
    high = value.astype(BF16)
    return high, (value - high.astype(F32)).astype(BF16)


def identity_of(width):
    rows = lax.broadcasted_iota(jnp.int32, (width, width), 0)
    columns = lax.broadcasted_iota(jnp.int32, (width, width), 1)
    return (rows == columns).astype(F32)


def inverses(matrices, bounds, identity):
    scales = [2.0 / (1.0 + bound) for bound in bounds]
    gaps = [(bound - 1.0) / (bound + 1.0) for bound in bounds]
    rests = [identity - scale * matrix for scale, matrix in zip(scales, matrices)]
    found = [scale * identity for scale in scales]
    for step in range(STEPS):
        for i, rest in enumerate(rests):
            factor = 2.0 / (2.0 - gaps[i] * gaps[i])
            if step == 0:
                found[i] = factor * (scales[i] * (identity + rest))
            else:
                found[i] = factor * (found[i] + dot(found[i], rest))
            if step + 1 < STEPS:
                rests[i] = (1.0 - factor) * identity + factor * dot(rest, rest)
            gaps[i] = gaps[i] * gaps[i] / (2.0 - gaps[i] * gaps[i])
    for i, matrix in enumerate(matrices):
        found[i] = found[i] + dot(found[i], identity - dot(matrix, found[i]))
    return found


def columns_of(lead_coupling, trail_coupling):
    identity = identity_of(lead_coupling.shape[0])
    lead_flipped, trail_flipped = lead_coupling.T, trail_coupling.T
    bounds = [
        1.0 + jnp.sum(coupling * coupling, keepdims=True)
        for coupling in (lead_coupling, trail_coupling)
    ]
    left, right = inverses(
        [
            identity + dot(lead_coupling, lead_flipped),
            identity + dot(trail_flipped, trail_coupling),
        ],
        bounds,
        identity,
    )
    return (
        (2.0 * left - identity, 2.0 * dot(lead_flipped, left)),
        (-2.0 * dot(trail_coupling, right), 2.0 * right - identity),
    )


def kernel(
    seats, group, lead_ref, act_ref, out_ref, held, raw, own, gram_out, gram_in, coup_out, coup_in,
    coup_own, coup_near, turn_own, up_send, up_recv, down_send, down_recv, raw_up_send, raw_up_recv,
    raw_down_send, raw_down_recv, ahead_up_send, ahead_up_recv, ahead_down_send, ahead_down_recv,
    relay_send, relay_recv, near_up_send, near_up_recv, near_down_send, near_down_recv,
    gram_send, gram_recv, coup_send, coup_recv,
):
    rows = act_ref.shape[0]
    width = act_ref.shape[1] // 2
    early_rows = rows // 2
    sizes = [early_rows // EARLY] * EARLY + [(rows - early_rows) // (CHUNKS - EARLY)] * (CHUNKS - EARLY)
    spans = [pl.ds(sum(sizes[:c]), sizes[c]) for c in range(CHUNKS)]
    band = width // group
    seat = lax.axis_index("pair")
    me = lax.axis_index("row")
    above = lax.rem(seat + 1, seats)
    below = lax.rem(seat + seats - 1, seats)
    first, final = seat == 0, seat == seats - 1
    swapped = lead_ref[0] == 1

    barrier = pltpu.get_barrier_semaphore()
    far_first = sorted(range(group), key=lambda step: abs(2 * step - group))
    for step in far_first[:-1]:
        pl.semaphore_signal(
            barrier, inc=1, device_id={"row": lax.rem(me + step, group)}, device_id_type=MESH
        )
    for condition, other in ((seat > 0, below), (seat < seats - 1, above)):
        @pl.when(condition)
        def _():
            for step in far_first:
                pl.semaphore_signal(
                    barrier, inc=1, device_id={"pair": other, "row": lax.rem(me + step, group)},
                    device_id_type=MESH,
                )
    beside = (seat > 0).astype(jnp.int32) + (seat < seats - 1).astype(jnp.int32)

    def part(c):
        return spans[c]

    def to(other, source, target, send, receive):
        return pltpu.make_async_remote_copy(
            src_ref=source, dst_ref=target, send_sem=send, recv_sem=receive,
            device_id={"pair": other}, device_id_type=MESH,
        )

    def up_copy(c):
        return to(above, own.at[0, 0, part(c)], held.at[0, 0, part(c)], up_send.at[c], up_recv.at[c])

    def down_copy(c):
        return to(
            below, own.at[0, 1, part(c)], held.at[0, 1, part(c)], down_send.at[c], down_recv.at[c]
        )

    def raw_up(slot, c):
        return to(
            above, held.at[slot, 0, part(c)], raw.at[slot, 0, part(c)],
            raw_up_send.at[c], raw_up_recv.at[slot, c],
        )

    def raw_down(slot, c):
        return to(
            below, held.at[slot, 1, part(c)], raw.at[slot, 1, part(c)],
            raw_down_send.at[c], raw_down_recv.at[slot, c],
        )

    def ahead_up(c):
        return to(
            above, held.at[1, 1, part(c)], own.at[1, 1, part(c)], ahead_up_send.at[c], ahead_up_recv.at[c]
        )

    def ahead_down(c):
        return to(
            below, held.at[1, 0, part(c)], own.at[1, 0, part(c)],
            ahead_down_send.at[c], ahead_down_recv.at[c],
        )

    def near(other, side, slot, step, send, receive):
        return pltpu.make_async_remote_copy(
            src_ref=coup_out, dst_ref=coup_near.at[slot, side, 0, step // 2],
            send_sem=send, recv_sem=receive.at[slot],
            device_id={"pair": other, "row": lax.rem(me + step, group)}, device_id_type=MESH,
        )

    def near_all(other, side, slot, send, receive):
        bands = coup_near.at[slot, side, 0]
        return to(other, bands, bands, send, receive.at[slot])

    mate = me + 1 - 2 * lax.rem(me, 2)

    def relay(slot, side):
        return pltpu.make_async_remote_copy(
            src_ref=coup_near.at[slot, side, 0], dst_ref=coup_near.at[slot, side, 1],
            send_sem=relay_send.at[side], recv_sem=relay_recv.at[slot, side],
            device_id={"row": mate}, device_id_type=MESH,
        )

    def near_assembled(slot, side):
        rows_of = []
        for k in range(group):
            lane = lax.rem(me // 2 - k // 2 + group // 2, group // 2)
            rows_of.append(coup_near[slot, side, lax.rem(me + k, 2), lane])
        return jnp.concatenate(rows_of, axis=0)

    def gram_part(leading, trailing, totals):
        lead_high, lead_low = halves(leading)
        trail_high, trail_low = halves(trailing)
        both = dot(
            jnp.concatenate([lead_high, lead_low], axis=1),
            jnp.concatenate([trail_high, trail_low], axis=1),
            ((0,), (0,)),
        )
        cross = both[:width, :width] + (both[:width, width:] + both[width:, :width])
        norms = [
            jnp.sum((block * block).reshape(-1, 8, width), axis=0) for block in (leading, trailing)
        ]
        new = (cross, *norms)
        return new if totals is None else tuple(a + b for a, b in zip(totals, new))

    sent = pl.ds(0, band + 2)
    gram_all = pltpu.make_async_remote_copy(
        src_ref=gram_out.at[pl.ds(1, group - 1), sent], dst_ref=gram_in.at[pl.ds(1, group - 1), sent],
        send_sem=gram_send, recv_sem=gram_recv,
        device_id={"row": lax.rem(me + 1, group)}, device_id_type=MESH,
    )
    coup_all = pltpu.make_async_remote_copy(
        src_ref=coup_in.at[pl.ds(1, group - 1)], dst_ref=coup_in.at[pl.ds(1, group - 1)],
        send_sem=coup_send, recv_sem=coup_recv,
        device_id={"row": lax.rem(me + 1, group)}, device_id_type=MESH,
    )

    def sum_stage(cross, norm_lead, norm_trail):
        norm_lead = jnp.sum(norm_lead, axis=0, keepdims=True)
        norm_trail = jnp.sum(norm_trail, axis=0, keepdims=True)
        line = lax.broadcasted_iota(jnp.int32, (8, width), 0)
        norms = jnp.where(line == 0, norm_lead, jnp.where(line == 1, norm_trail, 0.0))
        for k in range(group):
            gram_out[k, :band] = cross[k * band : (k + 1) * band]
            gram_out[k, band:] = norms

    def sum_send():
        for step in far_first[:-1]:
            other = lax.rem(me + step, group)
            pltpu.make_async_remote_copy(
                src_ref=gram_out.at[other, sent], dst_ref=gram_in.at[step, sent],
                send_sem=gram_send, recv_sem=gram_recv,
                device_id={"row": other}, device_id_type=MESH,
            ).start()

    def assembled(bands):
        return jnp.concatenate([bands[lax.rem(me - k + group, group)] for k in range(group)], axis=0)

    def sum_end(slot=None, meanwhile=None):
        total = gram_out[me, :band]
        norms = gram_out[me, band : band + 2]
        gram_all.wait_recv()
        for step in range(1, group):
            total = total + gram_in[step, :band]
            norms = norms + gram_in[step, band : band + 2]
        lane = lax.broadcasted_iota(jnp.int32, (band, width), 1)
        mine = lane == me * band + lax.broadcasted_iota(jnp.int32, (band, width), 0)
        column = jnp.sum(jnp.where(mine, norms[:1], 0.0), axis=1, keepdims=True)
        coup_out[...] = total / (column + norms[1:] + EPSILON)
        if slot is not None:
            even = [step for step in far_first if step % 2 == 0]
            for some in (even[: group // 4], even[group // 4 :]):
                @pl.when(seat < seats - 1)
                def _():
                    for step in some:
                        near(above, 0, slot, step, near_up_send, near_up_recv).start()

                @pl.when(seat > 0)
                def _():
                    for step in some:
                        near(below, 1, slot, step, near_down_send, near_down_recv).start()

        if meanwhile is not None:
            forward(slot, EARLY)
        for step in far_first[:-1]:
            pltpu.make_async_remote_copy(
                src_ref=coup_out, dst_ref=coup_in.at[step],
                send_sem=coup_send, recv_sem=coup_recv,
                device_id={"row": lax.rem(me + step, group)}, device_id_type=MESH,
            ).start()
        if meanwhile is not None:
            for c in range(EARLY + 1, CHUNKS):
                forward(slot, c)
            meanwhile()
        coup_in[0] = coup_out[...]
        coup_all.wait_recv()
        gram_all.wait_send()
        coup_all.wait_send()
        return assembled(coup_in)

    def turn(coupling, swap_rows, swap_columns):
        lead_columns, trail_columns = columns_of(coupling, coupling)
        top, bottom = (
            jnp.concatenate(pair, axis=1) for pair in zip(lead_columns, trail_columns)
        )
        if swap_rows:
            top, bottom = jnp.where(swapped, bottom, top), jnp.where(swapped, top, bottom)
        whole = jnp.concatenate([top, bottom], axis=0)
        if swap_columns:
            turned = jnp.concatenate([whole[:, width:], whole[:, :width]], axis=1)
            whole = jnp.where(first, turned, whole)
        return halves(whole)

    def applied(block, turn_high, turn_low):
        high, low = halves(block)
        return dot(high, turn_high) + (dot(high, turn_low) + dot(low, turn_high))

    def applied_half(block, turn_both):
        high, low = halves(block)
        both = dot(high, turn_both)
        return both[:, :width] + (both[:, width:] + dot(low, turn_both[:, :width]))

    def held_block(slot, c):
        return jnp.concatenate([held[slot, 0, part(c)], held[slot, 1, part(c)]], axis=1)

    def forward(slot, c):
        @pl.when(seat < seats - 1)
        def _():
            raw_up(slot, c).start()

        @pl.when(seat > 0)
        def _():
            raw_down(slot, c).start()

    def near_turns(now):
        @pl.when(first)
        def _():
            for lane in range(group // 2):
                coup_near[now, 0, 0, lane] = coup_in[2 * lane]
                other = lax.rem(me - mate + 2 * lane + group, group)
                coup_near[now, 0, 1, lane] = coup_in[other]

        @pl.when(final)
        def _():
            for lane in range(group // 2):
                coup_near[now, 1, 0, lane] = coup_in[2 * lane]
                other = lax.rem(me - mate + 2 * lane + group, group)
                coup_near[now, 1, 1, lane] = coup_in[other]

        @pl.when(seat > 0)
        def _():
            near_all(below, 0, now, near_down_send, near_up_recv).wait_recv()
            relay(now, 0).start()

        @pl.when(seat < seats - 1)
        def _():
            near_all(above, 1, now, near_up_send, near_down_recv).wait_recv()
            relay(now, 1).start()

        @pl.when(seat > 0)
        def _():
            near_all(below, 1, now, near_down_send, near_down_recv).wait_send()
            relay(now, 0).wait()

        @pl.when(seat < seats - 1)
        def _():
            near_all(above, 0, now, near_up_send, near_up_recv).wait_send()
            relay(now, 1).wait()

        low, high = near_assembled(now, 0), near_assembled(now, 1)
        (low_top, low_bottom), (high_top, high_bottom) = columns_of(
            jnp.where(seat == 1, -low.T, low), jnp.where(final, -high.T, high)
        )
        lead_turn = jnp.concatenate(
            [jnp.where(seat == 1, low_bottom, low_top), jnp.where(seat == 1, low_top, low_bottom)]
        )
        trail_turn = jnp.concatenate(
            [jnp.where(final, high_bottom, high_top), jnp.where(final, high_top, high_bottom)]
        )
        lead_turn = jnp.concatenate(halves(lead_turn), axis=1)
        trail_turn = jnp.concatenate(halves(trail_turn), axis=1)
        return lead_turn, trail_turn

    def near_chunk(now, c, turns):
        lead_turn, trail_turn = turns

        @pl.when(seat > 0)
        def _():
            raw_up(now, c).wait_recv()
            raw_down(now, c).wait_send()

        @pl.when(seat < seats - 1)
        def _():
            raw_down(now, c).wait_recv()
            raw_up(now, c).wait_send()

        leading = applied_half(
            jnp.concatenate([raw[now, 0, part(c)], own[now, 1, part(c)]], axis=1), lead_turn
        )
        trailing = applied_half(
            jnp.concatenate([own[now, 0, part(c)], raw[now, 1, part(c)]], axis=1), trail_turn
        )
        return leading, trailing

    def keep_at_ends(slot, c, leading, trailing):
        @pl.when(first)
        def _():
            raw[slot, 0, part(c)] = leading
            own[slot, 1, part(c)] = trailing

        @pl.when(final)
        def _():
            raw[slot, 1, part(c)] = trailing
            own[slot, 0, part(c)] = leading

    totals = None
    for c in range(CHUNKS):
        totals = gram_part(act_ref[part(c), :width], act_ref[part(c), width:], totals)
    cross, norm_first, norm_second = totals
    sum_stage(
        jnp.where(swapped, cross.T, cross),
        jnp.where(swapped, norm_second, norm_first),
        jnp.where(swapped, norm_first, norm_second),
    )
    for c in range(AHEAD):
        one, two = act_ref[part(c), :width], act_ref[part(c), width:]
        leading, trailing = jnp.where(swapped, two, one), jnp.where(swapped, one, two)
        held[1, 0, part(c)] = leading
        held[1, 1, part(c)] = trailing
        keep_at_ends(1, c, leading, trailing)

    pl.semaphore_wait(barrier, group - 1 + group * beside)
    sum_send()
    for c in range(AHEAD):
        forward(1, c)

        @pl.when(seat < seats - 1)
        def _():
            ahead_up(c).start()

        @pl.when(seat > 0)
        def _():
            ahead_down(c).start()

    turned = turn(sum_end(1), True, True)
    for c in (*range(AHEAD, CHUNKS), *range(AHEAD)):
        new = applied(act_ref[part(c)], *turned)
        own[0, 0, part(c)] = new[:, :width]
        own[0, 1, part(c)] = new[:, width:]
        if c >= AHEAD:
            @pl.when(seat < seats - 1)
            def _():
                up_copy(c).start()

            @pl.when(seat > 0)
            def _():
                down_copy(c).start()

            @pl.when(final)
            def _():
                held[0, 1, part(c)] = new[:, :width]

            @pl.when(first)
            def _():
                held[0, 0, part(c)] = new[:, width:]

    turns = near_turns(1)
    totals = None
    for c in range(CHUNKS):
        if c < AHEAD:
            @pl.when(seat > 0)
            def _():
                ahead_up(c).wait_recv()
                ahead_down(c).wait_send()

            @pl.when(seat < seats - 1)
            def _():
                ahead_down(c).wait_recv()
                ahead_up(c).wait_send()

            leading, trailing = near_chunk(1, c, turns)
            held[0, 0, part(c)] = leading
            held[0, 1, part(c)] = trailing
        else:
            @pl.when(seat > 0)
            def _():
                up_copy(c).wait_recv()
                down_copy(c).wait_send()

            @pl.when(seat < seats - 1)
            def _():
                down_copy(c).wait_recv()
                up_copy(c).wait_send()

            leading, trailing = held[0, 0, part(c)], held[0, 1, part(c)]
        if c < EARLY:
            forward(0, c)
        totals = gram_part(leading, trailing, totals)
        keep_at_ends(0, c, leading, trailing)

    def one_round(index, totals):
        now = lax.rem(index, 2)
        later = 1 - now
        sum_stage(*totals)
        sum_send()

        @pl.when(index > 2)
        def _():
            turn_own[0], turn_own[1] = turn(coup_own[...], False, True)

        def own_blocks():
            @pl.when(index > 2)
            def _():
                for c in range(CHUNKS):
                    new = applied(held_block(later, c), turn_own[0], turn_own[1])
                    own[now, 0, part(c)] = jnp.where(final, held[now, 0, part(c)], new[:, :width])
                    own[now, 1, part(c)] = jnp.where(first, held[now, 1, part(c)], new[:, width:])

        coup_own[...] = sum_end(now, own_blocks)

        turns = near_turns(now)
        totals = None
        for c in range(CHUNKS):
            leading, trailing = near_chunk(now, c, turns)
            held[later, 0, part(c)] = leading
            held[later, 1, part(c)] = trailing

            if c < EARLY:
                @pl.when(index < ROUNDS - 1)
                def _():
                    forward(later, c)

            @pl.when(first)
            def _():
                raw[later, 0, part(c)] = leading

            @pl.when(final)
            def _():
                raw[later, 1, part(c)] = trailing

            totals = gram_part(leading, trailing, totals)
        return totals

    totals = lax.fori_loop(2, ROUNDS, one_round, totals)
    last = ROUNDS % 2
    sum_stage(*totals)
    sum_send()
    turned = turn(sum_end(), False, False)
    for c in range(CHUNKS):
        out_ref[part(c)] = applied(held_block(last, c), *turned)


def shards(activations, lead):
    seats, group = lax.axis_size("pair"), lax.axis_size("row")
    rows, columns = activations.shape
    width = columns // 2
    band = width // group
    dma = pltpu.SemaphoreType.DMA
    return pl.pallas_call(
        functools.partial(kernel, seats, group),
        out_shape=jax.ShapeDtypeStruct((rows, columns), F32),
        in_specs=[
            pl.BlockSpec(memory_space=pltpu.SMEM),
            pl.BlockSpec(memory_space=pltpu.VMEM),
        ],
        out_specs=pl.BlockSpec(memory_space=pltpu.VMEM),
        scratch_shapes=[
            pltpu.VMEM((2, 2, rows, width), F32),
            pltpu.VMEM((2, 2, rows, width), F32),
            pltpu.VMEM((2, 2, rows, width), F32),
            pltpu.VMEM((group, band + 8, width), F32),
            pltpu.VMEM((group, band + 8, width), F32),
            pltpu.VMEM((band, width), F32),
            pltpu.VMEM((group, band, width), F32),
            pltpu.VMEM((width, width), F32),
            pltpu.VMEM((2, 2, 2, group // 2, band, width), F32),
            pltpu.VMEM((2, columns, columns), BF16),
            dma((CHUNKS,)),
            dma((CHUNKS,)),
            dma((CHUNKS,)),
            dma((CHUNKS,)),
            dma((CHUNKS,)),
            dma((2, CHUNKS)),
            dma((CHUNKS,)),
            dma((2, CHUNKS)),
            dma((AHEAD,)),
            dma((AHEAD,)),
            dma((AHEAD,)),
            dma((AHEAD,)),
            dma((2,)),
            dma((2, 2)),
            dma,
            dma((2,)),
            dma,
            dma((2,)),
            dma,
            dma,
            dma,
            dma,
        ],
        compiler_params=pltpu.CompilerParams(
            collective_id=0, has_side_effects=True, vmem_limit_bytes=48 * 1024 * 1024
        ),
        cost_estimate=pl.CostEstimate(
            flops=ROUNDS * 2 * rows * columns * (2 * columns + width),
            bytes_accessed=2 * rows * columns * 4,
            transcendentals=0,
        ),
    )(lead, activations)


def solution(mesh):
    return jax.shard_map(
        shards,
        mesh=mesh,
        in_specs=(P("row", "pair"), P("pair")),
        out_specs=P("row", "pair"),
        check_vma=False,
    )
```
